32 devices in a mesh: parts: 2 (over y), seq: 4 (over x, core), tensor: 4 (over z).
Axes of the slice: x: 2, y: 2, z: 4, core: 2. Of those that a mesh axis runs over, the one named last changes fastest.
Arguments:
- token_ids: int32 [2048], P(('parts', 'seq')), parts along dimension 0, may hold values from 0 to 511
- embed: bfloat16 [512, 8192], P(None, 'tensor'), may hold values from -6 to 6
- norm_gain_vector: float32 [8192], P('tensor'), may hold values from 0.25 to 1.75
- base_proj: bfloat16 [3, 2048, 8192], P(None, ('parts', 'seq'), 'tensor'), parts along dimension 1, may hold values from -6 to 6
- adapter_down_matrices: bfloat16 [8192, 384], P('tensor'), may hold values from -0.0625 to 0.0625
- adapter_up_matrices: bfloat16 [3, 128, 8192], P(None, None, 'tensor'), may hold values from -0.5 to 0.5
- short_taps: float32 [3, 7, 8192], P(None, None, 'tensor'), may hold values from -2 to 2
- medium_taps: float32 [128, 8192], P(None, 'tensor'), may hold values from -0.5 to 0.5
- skip_gain: float32 [8192], P('tensor'), may hold values from 0.25 to 1.75
- mixer_cot: bfloat16 [2048, 8192], P(('parts', 'seq'), 'tensor'), parts along dimension 0, may hold values from -6 to 6
- bucket_ids: int32 [8192], P('tensor'), may hold values from 0 to 31
Outputs:
- features: float32 [4, 16, 384], P('parts'), parts along dimension 0
The draws below stay inside these ranges and needn't reach their ends.
There are 2 independent parts, one for each index of `parts`. The reference program is written for one: setup_inputs(seed, part) draws one part's arguments, and reference() takes and returns one part's arrays. A program takes and returns all parts, laid end to end along the dimension named above; an argument that names none is the same for every part. Nothing has to cross between parts.
All inputs are finite; a program needn't handle non-finite values.
Results may differ from the reference program's by a relative error of at most 0.0069.
Values sent between devices are 32-bit elements; how exact they have to be, the bound alone decides.
A program may use at most 192 MiB of HBM per device.

```python
import jax
import jax.numpy as jnp
from jax import lax

D = 8192
V = 512
MEDIUM = 128
SHORT = 7
ADAPTER_RANKS = 128
BUCKETS = 16
SLAB_TOKENS = 1024


def touch_ends(drawn, rng, low, high):
    longest = drawn.shape.index(max(drawn.shape))
    spots = []
    for shift in (0, 1):
        where = [jax.random.randint(jax.random.fold_in(rng, axis), (), 0, length) for axis, length in enumerate(drawn.shape)]
        where[longest] = (where[longest] + shift) % drawn.shape[longest]
        spots.append(tuple(where))
    return drawn.at[spots[0]].set(low).at[spots[1]].set(high)


def shard_levels(key, extent, cuts, low, top_value):
    factor_of, own = 1.0, jax.random.fold_in(key, 6)
    for dim, shards_of in cuts:
        heights = jnp.exp(jax.random.uniform(jax.random.fold_in(own, dim), (shards_of,), jnp.float32, low / len(cuts), top_value / len(cuts)))
        factor_of = factor_of * jnp.repeat(heights, extent[dim] // shards_of).reshape([-1 if axis == dim else 1 for axis in range(len(extent))])
    return factor_of


def scatter_about(rng, shape, deviation, reach, shards=(), held_as=jnp.bfloat16):
    drawn = jax.random.normal(rng, shape, jnp.float32) * deviation
    if len(shards) > 0:
        drawn = shard_levels(rng, shape, shards, -0.22, 0.18) * drawn
    return jnp.clip(drawn, min=-reach, max=reach).astype(held_as)


def setup_inputs(seed: int = 0, part: int = 0) -> dict:
    seeds = jax.random.split(jax.random.key(seed), 12)
    part_splits = jax.random.split(jax.random.fold_in(seeds[11], part), 12)
    return {
        "token_ids": touch_ends(jax.random.randint(part_splits[0], (SLAB_TOKENS,), 0, V), jax.random.fold_in(part_splits[0], 1), 0, V - 1).astype(jnp.int32),
        "embed": scatter_about(seeds[1], (V, D), 1.0, 6.0, ((1, 4),)),
        "norm_gain_vector": jnp.clip(1.0 + 0.15 * jax.random.normal(seeds[2], (D,), jnp.float32), 0.25, 1.75),
        "base_proj": scatter_about(part_splits[3], (3, SLAB_TOKENS, D), 1.0, 6.0, ((1, 4), (2, 4))),
        "adapter_down_matrices": scatter_about(seeds[4], (D, 3 * ADAPTER_RANKS), D ** -0.5, 0.0625, ((0, 4),)),
        "adapter_up_matrices": scatter_about(seeds[5], (3, ADAPTER_RANKS, D), ADAPTER_RANKS ** -0.5, 0.5, ((2, 4),)),
        "short_taps": scatter_about(seeds[6], (3, SHORT, D), SHORT ** -0.5, 2.0, ((2, 4),), jnp.float32),
        "medium_taps": scatter_about(seeds[7], (MEDIUM, D), MEDIUM ** -0.5, 0.5, ((1, 4),), jnp.float32),
        "skip_gain": jnp.clip(1.0 + 0.15 * jax.random.normal(seeds[8], (D,), jnp.float32), 0.25, 1.75),
        "mixer_cot": scatter_about(part_splits[9], (SLAB_TOKENS, D), 1.0, 6.0, ((0, 4), (1, 4))),
        "bucket_ids": touch_ends(jax.random.randint(seeds[10], (D,), 0, 2 * BUCKETS), jax.random.fold_in(seeds[10], 1), 0, (2 * BUCKETS) - 1).astype(jnp.int32),
    }


NORM_EPS = 1e-05
FEATURE_EPS = 1e-06
ADAPTER_SCALE = 1.5

def causal_taps(field, filter_taps):
    tap_count = filter_taps.shape[0]
    length = field.shape[0]
    padded = jnp.pad(field, ((tap_count - 1, 0), (0, 0)))

    def one_tap(tap_index, running):
        offset = (tap_count - 1 - tap_index).astype(jnp.int32)
        return running + filter_taps[tap_index] * lax.dynamic_slice_in_dim(padded, offset, length, 0)
    return lax.fori_loop(0, tap_count, one_tap, jnp.zeros(field.shape, jnp.float32))

def anticausal_taps(field, filter_taps):
    tap_count = filter_taps.shape[0]
    length = field.shape[0]
    padded = jnp.pad(field, ((0, tap_count - 1), (0, 0)))

    def one_tap(tap_index, running):
        offset = jnp.asarray(tap_index).astype(jnp.int32)
        return running + filter_taps[tap_index] * lax.dynamic_slice_in_dim(padded, offset, length, 0)
    return lax.fori_loop(0, tap_count, one_tap, jnp.zeros(field.shape, jnp.float32))

def reference(token_ids, embed, norm_gain_vector, base_proj, adapter_down_matrices, adapter_up_matrices, short_taps, medium_taps, skip_gain, mixer_cot, bucket_ids):
    inputs = embed[token_ids].astype(jnp.float32)
    mean_square = lax.optimization_barrier(jnp.mean(inputs * inputs, axis=1, keepdims=True))
    norm_applied = (inputs * lax.rsqrt(mean_square + NORM_EPS) * norm_gain_vector).astype(jnp.bfloat16)
    rank_collapsed = (jnp.dot(norm_applied, adapter_down_matrices, preferred_element_type=jnp.float32) * ADAPTER_SCALE).astype(jnp.bfloat16)
    stream_reduced = rank_collapsed.reshape(SLAB_TOKENS, 3, ADAPTER_RANKS).astype(jnp.float32)
    block_width = min(D, 512)
    blocks = D // block_width

    def split_blocks(array):
        shaped = array.reshape(array.shape[:-1] + (blocks, block_width))
        return jnp.moveaxis(shaped, -2, 0)
    pieces_all = (split_blocks(base_proj), split_blocks(adapter_up_matrices), split_blocks(short_taps), split_blocks(medium_taps), split_blocks(skip_gain), split_blocks(mixer_cot))

    def per_block(gradient_low_rank, pieces):
        base_part, out_block, short_part, medium_part, skip_part, cot_part = pieces
        out_block = out_block.astype(jnp.float32)
        pre_mix = base_part.astype(jnp.float32) + jnp.einsum('tsr,src->stc', stream_reduced, out_block)
        filtered = [causal_taps(pre_mix[stream], short_part[stream]) for stream in range(3)]
        key_value = filtered[1] * filtered[2]
        mixed = causal_taps(key_value, medium_part) + skip_part * key_value
        cotangent = cot_part.astype(jnp.float32)
        grad_query = cotangent * mixed
        grad_mixed = cotangent * filtered[0]
        grad_kv = anticausal_taps(grad_mixed, medium_part) + skip_part * grad_mixed
        grad_key = grad_kv * filtered[2]
        grad_value = grad_kv * filtered[1]
        grad_streams = (grad_query, grad_key, grad_value)
        grad_pre = jnp.stack([anticausal_taps(grad_streams[stream], short_part[stream]) for stream in range(3)]).astype(jnp.bfloat16)
        grad_wide = grad_pre.astype(jnp.float32)
        grad_part = jnp.einsum('tsr,stc->src', stream_reduced, grad_wide)
        gradient_low_rank = gradient_low_rank + jnp.einsum('stc,src->tsr', grad_wide, out_block)
        return (gradient_low_rank, grad_part)
    gradient_low_rank, grad_parts = lax.scan(per_block, jnp.zeros((SLAB_TOKENS, 3, ADAPTER_RANKS), jnp.float32), pieces_all)
    grad_out = jnp.moveaxis(grad_parts, 0, 2).reshape(3 * ADAPTER_RANKS, D)
    gradient_low_rank = (gradient_low_rank.reshape(SLAB_TOKENS, 3 * ADAPTER_RANKS) * ADAPTER_SCALE).astype(jnp.bfloat16)
    grad_in = jnp.dot(norm_applied.T, gradient_low_rank, preferred_element_type=jnp.float32)
    buckets = bucket_ids % BUCKETS
    signs = jnp.where(bucket_ids >= BUCKETS, -1.0, 1.0).astype(jnp.float32)
    sketch_table = signs[:, None] * (buckets[:, None] == jnp.arange(BUCKETS, dtype=jnp.int32)[None, :]).astype(jnp.float32)
    sketch_in = jnp.dot(sketch_table.T, grad_in, precision=lax.Precision.HIGHEST)
    sketch_out = jnp.dot(sketch_table.T, grad_out.T, precision=lax.Precision.HIGHEST)
    raw = jnp.stack([sketch_in, sketch_out])
    return raw * lax.rsqrt(jnp.mean(raw * raw) + FEATURE_EPS)
```

```python
import jax
import jax.numpy as jnp
import numpy as np
from jax import lax
from jax.sharding import PartitionSpec as P

BUCKETS = 16
NORM_EPS = 1e-05
FEATURE_EPS = 1e-06
ADAPTER_SCALE = 1.5
RIM = 8
BF = jnp.bfloat16
F32 = jnp.float32


def from_behind(array, axis, by):
    count = lax.axis_size(axis)
    pairs = [(i, i + by) for i in range(count) if 0 <= i + by < count]
    return lax.ppermute(array, axis, pairs)


def spectrum_tables(rows, span):
    ext = rows + RIM + span
    half = -(-ext // 32) * 16
    period = 2 * half
    omega = 2.0 * np.pi * (np.arange(half) + 0.5) / period
    angle = omega[:, None] * np.arange(ext)[None, :]
    fwd = np.concatenate([np.cos(angle), -np.sin(angle)], axis=0)
    inv = fwd.T * (4.0 / period)
    return fwd, inv


def on_device(
    token_ids,
    embed,
    norm_gain_vector,
    base_proj,
    adapter_down_matrices,
    adapter_up_matrices,
    short_taps,
    medium_taps,
    skip_gain,
    mixer_cot,
    bucket_ids,
):
    rows = token_ids.shape[0]
    vocab = embed.shape[0]
    width = embed.shape[1]
    rank = adapter_up_matrices.shape[1]
    span = medium_taps.shape[0]
    taps = short_taps.shape[1]
    full = width * lax.axis_size("tensor")
    out_rows = rows + RIM

    ids = token_ids + 1
    ids_ext = jnp.concatenate(
        [from_behind(ids[rows - RIM :], "seq", 1), ids, from_behind(ids[:RIM], "seq", -1)]
    )
    base_ext = jnp.concatenate(
        [
            from_behind(base_proj[:, rows - RIM :].astype(F32), "seq", 1),
            base_proj.astype(F32),
            from_behind(base_proj[:, :RIM].astype(F32), "seq", -1),
        ],
        axis=1,
    )
    cot = mixer_cot.astype(F32)
    cot_ext = jnp.concatenate([cot, from_behind(cot[:RIM], "seq", -1)], axis=0)

    sketch = jnp.where(bucket_ids >= BUCKETS, -1.0, 1.0)[:, None] * (
        (bucket_ids % BUCKETS)[:, None] == jnp.arange(BUCKETS, dtype=jnp.int32)[None, :]
    )
    sketch = sketch.astype(BF)

    one_hot = (ids_ext[:, None] == 1 + jnp.arange(vocab, dtype=jnp.int32)[None, :]).astype(BF)
    inputs = jnp.dot(one_hot, embed, preferred_element_type=F32)
    squares = jnp.sum(inputs * inputs, axis=1, keepdims=True)
    gained = (inputs * norm_gain_vector).astype(BF)
    down = jnp.concatenate([adapter_down_matrices, sketch], axis=1)
    piece = jnp.dot(gained, down, preferred_element_type=F32)
    total = lax.psum(jnp.concatenate([piece, squares], axis=1), "tensor")
    scale = lax.rsqrt(total[:, -1:] / full + NORM_EPS)
    low = (total[:, : 3 * rank] * (scale * ADAPTER_SCALE)).astype(BF)
    token_sketch = (total[:, 3 * rank : -1] * scale)[RIM : RIM + rows]

    pre_mix = base_ext + jnp.einsum(
        "tsr,src->stc",
        low.reshape(-1, 3, rank),
        adapter_up_matrices,
        preferred_element_type=F32,
    )
    filtered = sum(
        short_taps[:, j][:, None, :] * pre_mix[:, RIM - j : RIM - j + out_rows]
        for j in range(taps)
    )
    key_value = filtered[1] * filtered[2]
    grad_mixed = cot_ext * filtered[0]
    kv_ext = jnp.concatenate(
        [from_behind(key_value[rows - span : rows], "seq", 1), key_value], axis=0
    )
    gm_ext = jnp.concatenate(
        [grad_mixed[:rows], from_behind(grad_mixed[: span + RIM], "seq", -1)], axis=0
    )

    fwd, inv = spectrum_tables(rows, span)
    half = fwd.shape[0] // 2
    fwd_t = jnp.asarray(fwd, BF)
    h = jnp.dot(fwd_t[:, :span], medium_taps.astype(BF), preferred_element_type=F32)
    x = jnp.dot(fwd_t, (kv_ext * 0.5).astype(BF), preferred_element_type=F32)
    g = jnp.dot(fwd_t, (gm_ext * 0.5).astype(BF), preferred_element_type=F32)
    hr, hi = h[:half], h[half:]
    xr, xi = x[:half], x[half:]
    gr, gi = g[:half], g[half:]
    y = jnp.concatenate([xr * hr - xi * hi, xr * hi + xi * hr], axis=0).astype(BF)
    z = jnp.concatenate([gr * hr + gi * hi, gi * hr - gr * hi], axis=0).astype(BF)
    mixed = (
        jnp.dot(jnp.asarray(inv[span : span + out_rows], BF), y, preferred_element_type=F32)
        + skip_gain * key_value
    )
    grad_kv = (
        jnp.dot(jnp.asarray(inv[:out_rows], BF), z, preferred_element_type=F32)
        + skip_gain * gm_ext[:out_rows]
    )
    streams = jnp.stack([cot_ext * mixed, grad_kv * filtered[2], grad_kv * filtered[1]])
    grad_pre = sum(
        short_taps[:, j][:, None, :] * streams[:, j : j + rows] for j in range(taps)
    ).astype(BF)

    wide = jnp.concatenate(
        [adapter_up_matrices, jnp.broadcast_to(sketch.T[None], (3, BUCKETS, width))], axis=1
    )
    prods = jnp.einsum("stc,skc->stk", grad_pre, wide, preferred_element_type=F32)
    sketch_in = ADAPTER_SCALE * jnp.einsum(
        "tk,str->ksr", token_sketch, prods[:, :, :rank], precision=lax.Precision.HIGHEST
    )
    sketch_out = jnp.einsum(
        "stk,tsr->ksr",
        prods[:, :, rank:],
        low[RIM : RIM + rows].reshape(rows, 3, rank).astype(F32),
        precision=lax.Precision.HIGHEST,
    )
    raw = jnp.stack([sketch_in, sketch_out]).reshape(2, BUCKETS, 3 * rank)
    raw = lax.psum(raw, ("seq", "tensor"))
    return raw * lax.rsqrt(jnp.mean(raw * raw) + FEATURE_EPS)


def solution(mesh):
    in_specs = (
        P(("parts", "seq")),
        P(None, "tensor"),
        P("tensor"),
        P(None, ("parts", "seq"), "tensor"),
        P("tensor", None),
        P(None, None, "tensor"),
        P(None, None, "tensor"),
        P(None, "tensor"),
        P("tensor"),
        P(("parts", "seq"), "tensor"),
        P("tensor"),
    )
    out_specs = P("parts", None, None)
    return jax.shard_map(
        on_device, mesh=mesh, in_specs=in_specs, out_specs=out_specs, check_vma=False
    )
```

```python
import functools

import jax
import jax.numpy as jnp
import numpy as np
from jax import lax
from jax.experimental import pallas as pl
from jax.experimental.pallas import tpu as pltpu
from jax.sharding import PartitionSpec as P

BUCKETS = 16
NORM_EPS = 1e-05
FEATURE_EPS = 1e-06
ADAPTER_SCALE = 1.5
RIM = 8
CHUNK = 256
BF = jnp.bfloat16
F32 = jnp.float32
HIGHEST = lax.Precision.HIGHEST
MESH = pl.DeviceIdType.MESH


def ceil_to(count, step):
    return -(-count // step) * step


def spectrum_tables(rows, span):
    ext = ceil_to(rows + RIM + span, 16)
    half = ceil_to(ext, 32) // 2
    period = 2 * half
    omega = 2.0 * np.pi * (np.arange(half) + 0.5) / period
    angle = omega[:, None] * np.arange(ext + 16)[None, :]
    fwd = np.concatenate([np.cos(angle), -np.sin(angle)], axis=0)
    inv = fwd.T * (2.0 / period)
    out_rows = ceil_to(rows + RIM, 16)
    return fwd[:, :ext], inv[span : span + out_rows], inv[:out_rows]


def nn(a, b):
    return jnp.dot(a, b, preferred_element_type=F32)


def nt(a, b):
    return lax.dot_general(a, b, (((1,), (1,)), ((), ())), preferred_element_type=F32)


def tn(a, b):
    return lax.dot_general(
        a, b, (((0,), (0,)), ((), ())), precision=HIGHEST, preferred_element_type=F32
    )


def kernel(
    ns,
    nz,
    ids_ref,
    embed_ref,
    gain_ref,
    base_hbm,
    down_ref,
    up_hbm,
    short_ref,
    medium_ref,
    skip_ref,
    cot_hbm,
    bucket_ref,
    fwd_ref,
    inv1_ref,
    inv2_ref,
    out_ref,
    ids_ext,
    one_hot,
    base,
    up,
    cot,
    sketch,
    to_prev,
    to_next,
    from_next,
    from_prev,
    acc,
    rs,
    low,
    psk,
    spec,
    kv,
    gm,
    fk,
    fv,
    prods,
    part_z,
    part_s,
    load_sem,
    rim_send,
    rim_recv,
    rs_send,
    rs_recv,
    ag_send,
    ag_recv,
    kv_send,
    kv_recv,
    gm_send,
    gm_recv,
    fz_send,
    fz_recv,
    fs_send,
    fs_recv,
):
    rows = ids_ref.shape[0]
    vocab, width = embed_ref.shape
    rank = up_hbm.shape[1]
    span = medium_ref.shape[0]
    taps = short_ref.shape[1]
    padded = acc.shape[0]
    own_rows = padded // nz
    out_rows = rows + RIM
    all_rows = rows + 2 * RIM
    ext = kv.shape[1]
    half = fwd_ref.shape[0] // 2
    chunks = width // CHUNK
    wide = 3 * rank
    s_me = lax.axis_index("seq")
    z_me = lax.axis_index("tensor")
    has_prev = s_me > 0
    has_next = s_me < ns - 1
    prev = {"seq": lax.rem(s_me + ns - 1, ns)}
    succ = {"seq": lax.rem(s_me + 1, ns)}

    loads = [
        pltpu.make_async_copy(src, dst, load_sem.at[i])
        for i, (src, dst) in enumerate([(base_hbm, base), (up_hbm, up), (cot_hbm, cot)])
    ]
    for load in loads:
        load.start()

    barrier = pltpu.get_barrier_semaphore()
    for d in range(1, ns):
        pl.semaphore_signal(
            barrier, inc=1, device_id={"seq": lax.rem(s_me + d, ns)}, device_id_type=MESH
        )
    for d in range(1, nz):
        pl.semaphore_signal(
            barrier, inc=1, device_id={"tensor": lax.rem(z_me + d, nz)}, device_id_type=MESH
        )
    pl.semaphore_wait(barrier, ns + nz - 2)

    def remote(src, dst, send, recv, device):
        return pltpu.make_async_remote_copy(
            src_ref=src,
            dst_ref=dst,
            send_sem=send,
            recv_sem=recv,
            device_id=device,
            device_id_type=MESH,
        )

    ids_to_next = remote(
        ids_ref.at[rows - RIM : rows], ids_ext.at[0:RIM], rim_send.at[0], rim_recv.at[0], succ
    )
    ids_to_prev = remote(
        ids_ref.at[0:RIM],
        ids_ext.at[RIM + rows : all_rows],
        rim_send.at[1],
        rim_recv.at[1],
        prev,
    )
    rim_to_next = remote(to_next, from_prev, rim_send.at[2], rim_recv.at[2], succ)
    rim_to_prev = remote(to_prev, from_next, rim_send.at[3], rim_recv.at[3], prev)

    @pl.when(has_next)
    def _():
        ids_to_next.start()

    @pl.when(has_prev)
    def _():
        ids_to_prev.start()

    @pl.when(jnp.logical_not(has_prev))
    def _():
        ids_ext[0:RIM] = jnp.zeros((RIM, 128), jnp.int32)
        from_prev[...] = jnp.zeros_like(from_prev)
        for k in range(chunks):
            kv[k, 0:span] = jnp.zeros((span, CHUNK), F32)

    @pl.when(jnp.logical_not(has_next))
    def _():
        ids_ext[RIM + rows : all_rows] = jnp.zeros((RIM, 128), jnp.int32)
        from_next[...] = jnp.zeros_like(from_next)
        for k in range(chunks):
            gm[k, rows : rows + span + RIM] = jnp.zeros((span + RIM, CHUNK), F32)

    tail = ext - (out_rows + span)
    if tail:
        for k in range(chunks):
            kv[k, ext - tail : ext] = jnp.zeros((tail, CHUNK), F32)
            gm[k, ext - tail : ext] = jnp.zeros((tail, CHUNK), F32)
    if padded > all_rows:
        ids_ext[all_rows:padded] = jnp.zeros((padded - all_rows, 128), jnp.int32)
    ids_ext[RIM : RIM + rows] = ids_ref[...]
    bucket = bucket_ref[...]
    hit = lax.broadcasted_iota(jnp.int32, (BUCKETS, width), 0) == jnp.bitwise_and(
        bucket, BUCKETS - 1
    )
    sign = jnp.where(bucket >= BUCKETS, -1.0, 1.0).astype(F32)
    sketch[...] = jnp.where(hit, sign, 0.0).astype(BF)
    acc[...] = jnp.zeros_like(acc)
    prods[...] = jnp.zeros_like(prods)

    loads[0].wait()
    loads[2].wait()
    for s in range(3):
        to_prev[s] = base[s, 0 : 2 * RIM].astype(F32)[:RIM]
        to_next[s] = base[s, rows - 2 * RIM : rows].astype(F32)[RIM:]
    to_prev[3] = cot[0 : 2 * RIM].astype(F32)[:RIM]

    @pl.when(has_next)
    def _():
        rim_to_next.start()

    @pl.when(has_prev)
    def _():
        rim_to_prev.start()

    @pl.when(has_prev)
    def _():
        ids_to_next.wait_recv()

    @pl.when(has_next)
    def _():
        ids_to_prev.wait_recv()

    ids = jnp.concatenate([ids_ext[...]] * (vocab // 128), axis=1)
    one_hot[...] = jnp.where(
        ids == lax.broadcasted_iota(jnp.int32, (padded, vocab), 1) + 1, 1.0, 0.0
    ).astype(BF)

    def at(k):
        return pl.ds(pl.multiple_of(k * CHUNK, CHUNK), CHUNK)

    def front(k, carry):
        cols = at(k)
        x = nn(one_hot[...], embed_ref[:, cols])
        squares = jnp.sum(x * x, axis=1, keepdims=True)
        gained = x * gain_ref[:, cols]
        high = gained.astype(BF)
        rest = (gained - high.astype(F32)).astype(BF)
        weights = down_ref[cols, :]
        acc[:, :wide] += nn(high, weights) + nn(rest, weights)
        table = sketch[:, cols]
        acc[:, wide : wide + BUCKETS] += nt(high, table) + nt(rest, table)
        acc[:, wide + BUCKETS : wide + BUCKETS + 1] += squares
        return carry

    lax.fori_loop(0, chunks, front, 0)

    def rows_of(z):
        return pl.ds(pl.multiple_of(z * own_rows, 8), own_rows)

    mine = rows_of(z_me)
    scatters = []
    for d in range(1, nz):
        z_to = lax.rem(z_me + d, nz)
        scatters.append(
            remote(
                acc.at[rows_of(z_to)],
                rs.at[d - 1],
                rs_send.at[d - 1],
                rs_recv.at[d - 1],
                {"tensor": z_to},
            )
        )
    for copy in scatters:
        copy.start()

    def filter_spectrum(k, carry):
        spec[k] = nn(fwd_ref[:, :span], medium_ref[:, at(k)].astype(BF))
        return carry

    lax.fori_loop(0, chunks, filter_spectrum, 0)

    total = acc[mine, :]
    for d in range(1, nz):
        scatters[d - 1].wait_recv()
        total = total + rs[d - 1]
    scale = lax.rsqrt(
        total[:, wide + BUCKETS : wide + BUCKETS + 1] / (width * nz) + NORM_EPS
    )
    low[mine, :] = (total[:, :wide] * (scale * ADAPTER_SCALE)).astype(BF).astype(F32)
    psk[mine, :] = total[:, wide:] * scale
    gathers = []
    for d in range(1, nz):
        peer = {"tensor": lax.rem(z_me + d, nz)}
        gathers.append(
            remote(
                low.at[mine], low.at[mine], ag_send.at[0, d - 1], ag_recv.at[0, d - 1], peer
            )
        )
    for d in range(1, nz):
        peer = {"tensor": lax.rem(z_me + d, nz)}
        gathers.append(
            remote(
                psk.at[mine], psk.at[mine], ag_send.at[1, d - 1], ag_recv.at[1, d - 1], peer
            )
        )
    for copy in gathers:
        copy.start()

    loads[1].wait()

    @pl.when(has_prev)
    def _():
        rim_to_next.wait_recv()

    @pl.when(has_next)
    def _():
        rim_to_prev.wait_recv()

    for copy in gathers[: nz - 1]:
        copy.wait_recv()

    def kv_copy(k):
        return remote(
            kv.at[k, rows : rows + span], kv.at[k, 0:span], kv_send.at[k], kv_recv.at[k], succ
        )

    def gm_copy(k):
        return remote(
            gm.at[k, 0 : span + RIM],
            gm.at[k, rows : rows + span + RIM],
            gm_send.at[k],
            gm_recv.at[k],
            prev,
        )

    def streams_in(k, carry):
        cols = at(k)
        filtered = []
        for s in range(3):
            pre = jnp.concatenate(
                [from_prev[s, :, cols], base[s, :, cols].astype(F32), from_next[s, :, cols]],
                axis=0,
            ) + nn(low[0:all_rows, s * rank : (s + 1) * rank].astype(BF), up[s, :, cols])
            coeff = short_ref[s, :, cols]
            running = coeff[0:1] * pre[RIM : RIM + out_rows]
            for j in range(1, taps):
                running = running + coeff[j : j + 1] * pre[RIM - j : RIM - j + out_rows]
            filtered.append(running)
        fk[k] = filtered[1]
        fv[k] = filtered[2]
        kv[k, span : span + out_rows] = filtered[1] * filtered[2]
        gm[k, 0:rows] = cot[:, cols].astype(F32) * filtered[0][0:rows]

        @pl.when(has_next)
        def _():
            kv_copy(k).start()

        @pl.when(has_prev)
        def _():
            gm_copy(k).start()

        return carry

    lax.fori_loop(0, chunks, streams_in, 0)

    def streams_back(k, carry):
        cols = at(k)

        @pl.when(has_prev)
        def _():
            kv_copy(k).wait_recv()

        @pl.when(has_next)
        def _():
            gm_copy(k).wait_recv()

        hr, hi = spec[k, 0:half], spec[k, half:]
        x = nn(fwd_ref[...], kv[k].astype(BF))
        xr, xi = x[:half], x[half:]
        y = jnp.concatenate([xr * hr - xi * hi, xr * hi + xi * hr], axis=0).astype(BF)
        skip = skip_ref[:, cols]
        mixed = nn(inv1_ref[...], y)[:out_rows] + skip * kv[k, span : span + out_rows]
        g = nn(fwd_ref[...], gm[k].astype(BF))
        gr, gi = g[:half], g[half:]
        w = jnp.concatenate([gr * hr + gi * hi, gi * hr - gr * hi], axis=0).astype(BF)
        grad_kv = nn(inv2_ref[...], w)[:out_rows] + skip * gm[k, 0:out_rows]
        cot_ext = jnp.concatenate([cot[:, cols].astype(F32), from_next[3, :, cols]], axis=0)
        table = sketch[:, cols]
        for s in range(3):
            if s == 0:
                stream = cot_ext * mixed
            elif s == 1:
                stream = grad_kv * fv[k]
            else:
                stream = grad_kv * fk[k]
            coeff = short_ref[s, :, cols]
            running = coeff[0:1] * stream[0:rows]
            for j in range(1, taps):
                running = running + coeff[j : j + 1] * stream[j : j + rows]
            joined = jnp.concatenate([up[s, :, cols], table], axis=0)
            prods[s] += nt(running.astype(BF), joined)
        return carry

    lax.fori_loop(0, chunks, streams_back, 0)

    for copy in gathers[nz - 1 :]:
        copy.wait_recv()
    token_sketch = psk[RIM : RIM + rows, 0:BUCKETS]
    for s in range(3):
        block = slice(s * rank, (s + 1) * rank)
        part_z[z_me, 0:BUCKETS, block] = ADAPTER_SCALE * tn(token_sketch, prods[s, :, 0:rank])
        part_z[z_me, BUCKETS : 2 * BUCKETS, block] = tn(
            prods[s, :, rank:], low[RIM : RIM + rows, block]
        )

    def share(buffer, me, count, axis, send, recv):
        copies = [
            remote(
                buffer.at[me],
                buffer.at[me],
                send.at[d - 1],
                recv.at[d - 1],
                {axis: lax.rem(me + d, count)},
            )
            for d in range(1, count)
        ]
        for copy in copies:
            copy.start()
        for copy in copies:
            copy.wait_recv()
        total = buffer[0]
        for i in range(1, count):
            total = total + buffer[i]
        return total, copies

    total, sent_z = share(part_z, z_me, nz, "tensor", fz_send, fz_recv)
    part_s[s_me] = total
    raw, sent_s = share(part_s, s_me, ns, "seq", fs_send, fs_recv)
    mean = jnp.sum(raw * raw) / (2 * BUCKETS * wide)
    features = raw * lax.rsqrt(jnp.full((1, wide), FEATURE_EPS, F32) + mean)
    out_ref[0] = features[:BUCKETS]
    out_ref[1] = features[BUCKETS:]

    for copy in scatters + gathers + sent_z + sent_s:
        copy.wait_send()

    @pl.when(has_next)
    def _():
        ids_to_next.wait_send()
        rim_to_next.wait_send()

        def drain(k, carry):
            kv_copy(k).wait_send()
            return carry

        lax.fori_loop(0, chunks, drain, 0)

    @pl.when(has_prev)
    def _():
        ids_to_prev.wait_send()
        rim_to_prev.wait_send()

        def drain(k, carry):
            gm_copy(k).wait_send()
            return carry

        lax.fori_loop(0, chunks, drain, 0)


def on_device(
    ns,
    nz,
    token_ids,
    embed,
    norm_gain_vector,
    base_proj,
    adapter_down_matrices,
    adapter_up_matrices,
    short_taps,
    medium_taps,
    skip_gain,
    mixer_cot,
    bucket_ids,
):
    rows = token_ids.shape[0]
    vocab, width = embed.shape
    rank = adapter_up_matrices.shape[1]
    span = medium_taps.shape[0]
    wide = 3 * rank
    chunks = width // CHUNK
    fwd, inv1, inv2 = spectrum_tables(rows, span)
    ext = fwd.shape[1]
    out_rows = rows + RIM
    padded = ceil_to(rows + 2 * RIM, 16 * nz)
    ids = jnp.broadcast_to(token_ids[:, None] + 1, (rows, 128))
    vmem = pl.BlockSpec(memory_space=pltpu.VMEM)
    any_space = pl.BlockSpec(memory_space=pl.ANY)
    dma = pltpu.SemaphoreType.DMA
    return pl.pallas_call(
        functools.partial(kernel, ns, nz),
        out_shape=jax.ShapeDtypeStruct((2, BUCKETS, wide), F32),
        in_specs=[vmem, vmem, vmem, any_space, vmem, any_space, vmem, vmem, vmem, any_space]
        + [vmem] * 4,
        out_specs=vmem,
        scratch_shapes=[
            pltpu.VMEM((padded, 128), jnp.int32),
            pltpu.VMEM((padded, vocab), BF),
            pltpu.VMEM((3, rows, width), BF),
            pltpu.VMEM((3, rank, width), BF),
            pltpu.VMEM((rows, width), BF),
            pltpu.VMEM((BUCKETS, width), BF),
            pltpu.VMEM((4, RIM, width), F32),
            pltpu.VMEM((3, RIM, width), F32),
            pltpu.VMEM((4, RIM, width), F32),
            pltpu.VMEM((3, RIM, width), F32),
            pltpu.VMEM((padded, wide + 128), F32),
            pltpu.VMEM((nz - 1, padded // nz, wide + 128), F32),
            pltpu.VMEM((padded, wide), F32),
            pltpu.VMEM((padded, 128), F32),
            pltpu.VMEM((chunks, fwd.shape[0], CHUNK), F32),
            pltpu.VMEM((chunks, ext, CHUNK), F32),
            pltpu.VMEM((chunks, ext, CHUNK), F32),
            pltpu.VMEM((chunks, out_rows, CHUNK), F32),
            pltpu.VMEM((chunks, out_rows, CHUNK), F32),
            pltpu.VMEM((3, rows, rank + BUCKETS), F32),
            pltpu.VMEM((nz, 2 * BUCKETS, wide), F32),
            pltpu.VMEM((ns, 2 * BUCKETS, wide), F32),
            dma((3,)),
            dma((4,)),
            dma((4,)),
            dma((nz - 1,)),
            dma((nz - 1,)),
            dma((2, nz - 1)),
            dma((2, nz - 1)),
            dma((chunks,)),
            dma((chunks,)),
            dma((chunks,)),
            dma((chunks,)),
            dma((nz - 1,)),
            dma((nz - 1,)),
            dma((ns - 1,)),
            dma((ns - 1,)),
        ],
        compiler_params=pltpu.CompilerParams(
            collective_id=0, has_side_effects=True, vmem_limit_bytes=52 * 1024 * 1024
        ),
    )(
        ids,
        embed,
        norm_gain_vector[None],
        base_proj,
        adapter_down_matrices,
        adapter_up_matrices,
        short_taps,
        medium_taps,
        skip_gain[None],
        mixer_cot,
        bucket_ids[None],
        jnp.asarray(fwd, BF),
        jnp.asarray(inv1, BF),
        jnp.asarray(inv2, BF),
    )


def solution(mesh):
    in_specs = (
        P(("parts", "seq")),
        P(None, "tensor"),
        P("tensor"),
        P(None, ("parts", "seq"), "tensor"),
        P("tensor", None),
        P(None, None, "tensor"),
        P(None, None, "tensor"),
        P(None, "tensor"),
        P("tensor"),
        P(("parts", "seq"), "tensor"),
        P("tensor"),
    )
    return jax.shard_map(
        functools.partial(on_device, mesh.shape["seq"], mesh.shape["tensor"]),
        mesh=mesh,
        in_specs=in_specs,
        out_specs=P("parts", None, None),
        check_vma=False,
    )
```

```python
import functools

import jax
import jax.numpy as jnp
import numpy as np
from jax import lax
from jax.experimental import pallas as pl
from jax.experimental.pallas import tpu as pltpu
from jax.sharding import PartitionSpec as P

BUCKETS = 16
NORM_EPS = 1e-05
FEATURE_EPS = 1e-06
ADAPTER_SCALE = 1.5
RIM = 8
CHUNK = 256
BF = jnp.bfloat16
F32 = jnp.float32
HIGHEST = lax.Precision.HIGHEST
MESH = pl.DeviceIdType.MESH


def ceil_to(count, step):
    return -(-count // step) * step


def spectrum_tables(rows, span):
    ext = ceil_to(rows + RIM + span, 16)
    half = ceil_to(ext, 32) // 2
    period = 2 * half
    omega = 2.0 * np.pi * (np.arange(half) + 0.5) / period
    angle = omega[:, None] * np.arange(ext + 16)[None, :]
    fwd = np.concatenate([np.cos(angle), -np.sin(angle)], axis=0)
    inv = fwd.T * (2.0 / period)
    out_rows = ceil_to(rows + RIM, 16)
    return fwd[:, :ext], inv[span : span + out_rows], inv[:out_rows]


def nn(a, b):
    return jnp.dot(a, b, preferred_element_type=F32)


def nt(a, b):
    return lax.dot_general(a, b, (((1,), (1,)), ((), ())), preferred_element_type=F32)


def tn(a, b):
    return lax.dot_general(
        a, b, (((0,), (0,)), ((), ())), precision=HIGHEST, preferred_element_type=F32
    )


def kernel(
    npart,
    ns,
    nz,
    ids_ref,
    embed_hbm,
    gain_hbm,
    base_hbm,
    down_hbm,
    up_hbm,
    short_hbm,
    medium_hbm,
    skip_hbm,
    cot_hbm,
    bucket_hbm,
    fwd_hbm,
    inv1_hbm,
    inv2_hbm,
    out_ref,
    embed_own,
    gain_ref,
    base,
    down_ref,
    up,
    short_ref,
    medium_ref,
    skip_ref,
    cot,
    bucket_ref,
    fwd_ref,
    inv1_ref,
    inv2_ref,
    ids_ext,
    sketch,
    to_prev,
    to_next,
    from_next,
    from_prev,
    acc,
    sums,
    rs,
    tab,
    ptab,
    flat,
    pflat,
    low,
    psk,
    spec,
    kv,
    gm,
    fk,
    fv,
    shift,
    prods,
    part,
    got_s,
    got_z,
    full_sum,
    done,
    load_sem,
    rim_send,
    rim_recv,
    rs_send,
    rs_recv,
    ag_send,
    ag_recv,
    pl_send,
    pl_recv,
    sib_send,
    sib_recv,
    kv_send,
    kv_recv,
    gm_send,
    gm_recv,
    fin_send,
    fin_recv,
    fz_send,
    fz_recv,
):
    rows = ids_ref.shape[0]
    vocab, width = embed_hbm.shape
    rank = up_hbm.shape[1]
    span = medium_ref.shape[0]
    taps = short_ref.shape[1]
    padded = ids_ext.shape[0]
    words = embed_own.shape[0]
    own = words // nz
    out_rows = rows + RIM
    all_rows = rows + 2 * RIM
    ext = kv.shape[1]
    half = fwd_ref.shape[0] // 2
    chunks = width // CHUNK
    wide = 3 * rank
    s_me = lax.axis_index("seq")
    z_me = lax.axis_index("tensor")
    p_me = lax.axis_index("parts")
    core = lax.rem(s_me, 2)
    sibling = {"seq": s_me + 1 - 2 * core}
    has_prev = s_me > 0
    has_next = s_me < ns - 1
    prev = {"seq": lax.rem(s_me + ns - 1, ns)}
    succ = {"seq": lax.rem(s_me + 1, ns)}

    first_word = pl.multiple_of((p_me * ns + s_me) * words, words)
    loads = [
        pltpu.make_async_copy(src, dst, load_sem.at[i])
        for i, (src, dst) in enumerate(
            [
                (embed_hbm.at[pl.ds(first_word, words)], embed_own),
                (gain_hbm, gain_ref),
                (bucket_hbm, bucket_ref),
                (down_hbm, down_ref),
                (base_hbm, base),
                (cot_hbm, cot),
                (fwd_hbm, fwd_ref),
                (medium_hbm, medium_ref),
                (up_hbm, up),
                (short_hbm, short_ref),
                (skip_hbm, skip_ref),
                (inv1_hbm, inv1_ref),
                (inv2_hbm, inv2_ref),
            ]
        )
    ]
    for load in loads:
        load.start()

    barrier = pltpu.get_barrier_semaphore()
    for d in range(1, ns):
        pl.semaphore_signal(
            barrier, inc=1, device_id={"seq": lax.rem(s_me + d, ns)}, device_id_type=MESH
        )
    for d in range(1, nz):
        pl.semaphore_signal(
            barrier, inc=1, device_id={"tensor": lax.rem(z_me + d, nz)}, device_id_type=MESH
        )
    plane = [(dp, ds) for dp in range(npart) for ds in range(0, ns, 2)][1:]

    def plane_peer(dp, ds):
        return lax.rem(p_me + dp, npart), lax.rem(s_me + ds, ns)

    away = [(dp, ds) for dp, ds in plane if dp > 0]
    for dp, ds in away:
        p_to, s_to = plane_peer(dp, ds)
        pl.semaphore_signal(
            barrier, inc=1, device_id={"parts": p_to, "seq": s_to}, device_id_type=MESH
        )
    pl.semaphore_wait(barrier, ns + nz - 2 + len(away))

    def remote(src, dst, send, recv, device):
        return pltpu.make_async_remote_copy(
            src_ref=src,
            dst_ref=dst,
            send_sem=send,
            recv_sem=recv,
            device_id=device,
            device_id_type=MESH,
        )

    ids_to_next = remote(
        ids_ref.at[rows - RIM : rows], ids_ext.at[0:RIM], rim_send.at[0], rim_recv.at[0], succ
    )
    ids_to_prev = remote(
        ids_ref.at[0:RIM],
        ids_ext.at[RIM + rows : all_rows],
        rim_send.at[1],
        rim_recv.at[1],
        prev,
    )
    rim_to_next = remote(to_next, from_prev, rim_send.at[2], rim_recv.at[2], succ)
    rim_to_prev = remote(to_prev, from_next, rim_send.at[3], rim_recv.at[3], prev)

    @pl.when(has_next)
    def _():
        ids_to_next.start()

    @pl.when(has_prev)
    def _():
        ids_to_prev.start()

    @pl.when(jnp.logical_not(has_prev))
    def _():
        ids_ext[0:RIM] = jnp.zeros((RIM, 128), jnp.int32)
        from_prev[...] = jnp.zeros_like(from_prev)
        for k in range(chunks):
            kv[k, 0:span] = jnp.zeros((span, CHUNK), F32)

    @pl.when(jnp.logical_not(has_next))
    def _():
        ids_ext[RIM + rows : all_rows] = jnp.zeros((RIM, 128), jnp.int32)
        from_next[...] = jnp.zeros_like(from_next)
        for k in range(chunks):
            gm[k, rows : rows + span + RIM] = jnp.zeros((span + RIM, CHUNK), F32)

    tail = ext - (out_rows + span)
    if tail:
        for k in range(chunks):
            kv[k, ext - tail : ext] = jnp.zeros((tail, CHUNK), F32)
            gm[k, ext - tail : ext] = jnp.zeros((tail, CHUNK), F32)
    if padded > all_rows:
        ids_ext[all_rows:padded] = jnp.zeros((padded - all_rows, 128), jnp.int32)
    ids_ext[RIM : RIM + rows] = ids_ref[...]
    for load in loads[:4]:
        load.wait()
    bucket = bucket_ref[...]
    hit = lax.broadcasted_iota(jnp.int32, (BUCKETS, width), 0) == jnp.bitwise_and(
        bucket, BUCKETS - 1
    )
    sign = jnp.where(bucket >= BUCKETS, -1.0, 1.0).astype(F32)
    sketch[...] = jnp.where(hit, sign, 0.0).astype(BF)
    sums[...] = jnp.zeros_like(sums)
    prods[...] = jnp.zeros_like(prods)

    def at(k):
        return pl.ds(pl.multiple_of(k * CHUNK, CHUNK), CHUNK)

    def front(k, carry):
        cols = at(k)
        x = embed_own[:, cols].astype(F32)
        squares = jnp.sum(x * x, axis=1, keepdims=True)
        gained = x * gain_ref[:, cols]
        high = gained.astype(BF)
        rest = (gained - high.astype(F32)).astype(BF)
        weights = down_ref[cols, :]
        sums[:, :wide] += nn(high, weights) + nn(rest, weights)
        table = sketch[:, cols]
        sums[:, wide : wide + BUCKETS] += nt(high, table) + nt(rest, table)
        sums[:, wide + BUCKETS : wide + BUCKETS + 1] += squares
        return carry

    lax.fori_loop(0, chunks, front, 0)

    for z in range(nz):
        acc[z] = sums[z * own : (z + 1) * own]
    scatters = []
    for d in range(1, nz):
        z_to = lax.rem(z_me + d, nz)
        scatters.append(
            remote(
                acc.at[z_to],
                rs.at[d - 1],
                rs_send.at[d - 1],
                rs_recv.at[d - 1],
                {"tensor": z_to},
            )
        )
    for copy in scatters:
        copy.start()

    loads[4].wait()
    loads[5].wait()
    for s in range(3):
        to_prev[s] = base[s, 0 : 2 * RIM].astype(F32)[:RIM]
        to_next[s] = base[s, rows - 2 * RIM : rows].astype(F32)[RIM:]
    to_prev[3] = cot[0 : 2 * RIM].astype(F32)[:RIM]

    @pl.when(has_next)
    def _():
        rim_to_next.start()

    @pl.when(has_prev)
    def _():
        rim_to_prev.start()


    total = acc[z_me]
    for d in range(1, nz):
        scatters[d - 1].wait_recv()
        total = total + rs[d - 1]
    scale = lax.rsqrt(
        total[:, wide + BUCKETS : wide + BUCKETS + 1] / (width * nz) + NORM_EPS
    )
    tab[p_me, s_me, z_me] = (total[:, :wide] * (scale * ADAPTER_SCALE)).astype(BF).astype(F32)
    ptab[p_me, s_me, z_me] = total[:, wide:] * scale

    def hand_out(which, buffer):
        lines, planes, siblings = [], [], []
        block = buffer.at[p_me, s_me, z_me]
        for d in range(1, nz):
            lines.append(
                remote(
                    block,
                    block,
                    ag_send.at[which, d - 1],
                    ag_recv.at[which, d - 1],
                    {"tensor": lax.rem(z_me + d, nz)},
                )
            )
        block = buffer.at[p_me, s_me]
        for i, (dp, ds) in enumerate(plane):
            p_to, s_to = plane_peer(dp, ds)
            planes.append(
                remote(
                    block,
                    block,
                    pl_send.at[which, i],
                    pl_recv.at[which, i],
                    {"parts": p_to, "seq": s_to},
                )
            )
        for i, (dp, ds) in enumerate([(0, 0)] + plane):
            p_of, s_of = lax.rem(p_me + npart - dp, npart), lax.rem(s_me + ns - ds, ns)
            block = buffer.at[p_of, s_of]
            siblings.append(
                remote(block, block, sib_send.at[which, i], sib_recv.at[which, i], sibling)
            )
        return lines, planes, siblings

    low_copies = hand_out(0, tab)
    psk_copies = hand_out(1, ptab)
    for copy in low_copies[0]:
        copy.start()
    for copy in psk_copies[0]:
        copy.start()

    for load in loads[6:]:
        load.wait()

    def filter_spectrum(k, carry):
        spec[k] = nn(fwd_ref[:, :span], medium_ref[:, at(k)].astype(BF))
        return carry

    for copy in low_copies[0]:
        copy.wait_recv()
    for copy in low_copies[1]:
        copy.start()
    low_copies[2][0].start()

    lax.fori_loop(0, chunks, filter_spectrum, 0)

    @pl.when(has_prev)
    def _():
        ids_to_next.wait_recv()
        rim_to_next.wait_recv()

    @pl.when(has_next)
    def _():
        ids_to_prev.wait_recv()
        rim_to_prev.wait_recv()

    ids = jnp.concatenate([ids_ext[...]] * (vocab // 128), axis=1)
    one_hot = jnp.where(
        ids == lax.broadcasted_iota(jnp.int32, (padded, vocab), 1) + 1, 1.0, 0.0
    ).astype(BF)

    for i, copy in enumerate(low_copies[1]):
        copy.wait_recv()
        low_copies[2][i + 1].start()
    for copy in psk_copies[0]:
        copy.wait_recv()
    for copy in psk_copies[1]:
        copy.start()
    psk_copies[2][0].start()
    for copy in low_copies[2]:
        copy.wait_recv()

    def flatten(buffer, target):
        for p in range(npart):
            for q in range(ns):
                for z in range(nz):
                    begin = ((p * ns + q) * nz + z) * own
                    target[begin : begin + own] = buffer[p, q, z]

    flatten(tab, flat)
    psk[...] = one_hot
    low[...] = nn(one_hot, flat[...].astype(BF)).astype(BF)

    def kv_copy(k):
        return remote(
            kv.at[k, rows : rows + span], kv.at[k, 0:span], kv_send.at[k], kv_recv.at[k], succ
        )

    def gm_copy(k):
        return remote(
            gm.at[k, 0 : span + RIM],
            gm.at[k, rows : rows + span + RIM],
            gm_send.at[k],
            gm_recv.at[k],
            prev,
        )

    def streams_in(k, carry):
        cols = at(k)
        filtered = []
        for s in range(3):
            shift[0:all_rows] = jnp.concatenate(
                [from_prev[s, :, cols], base[s, :, cols].astype(F32), from_next[s, :, cols]],
                axis=0,
            ) + nn(low[0:all_rows, s * rank : (s + 1) * rank], up[s, :, cols])
            coeff = short_ref[s, :, cols]
            running = coeff[0:1] * shift[RIM : RIM + out_rows]
            for j in range(1, taps):
                running = running + coeff[j : j + 1] * shift[RIM - j : RIM - j + out_rows]
            filtered.append(running)
        fk[k] = filtered[1]
        fv[k] = filtered[2]
        kv[k, span : span + out_rows] = filtered[1] * filtered[2]
        gm[k, 0:rows] = cot[:, cols].astype(F32) * filtered[0][0:rows]

        @pl.when(has_next)
        def _():
            kv_copy(k).start()

        @pl.when(has_prev)
        def _():
            gm_copy(k).start()

        return carry

    lax.fori_loop(0, chunks, streams_in, 0)

    def streams_back(k, carry):
        cols = at(k)

        @pl.when(has_prev)
        def _():
            kv_copy(k).wait_recv()

        @pl.when(has_next)
        def _():
            gm_copy(k).wait_recv()

        hr, hi = spec[k, 0:half], spec[k, half:]
        x = nn(fwd_ref[...], kv[k].astype(BF))
        xr, xi = x[:half], x[half:]
        y = jnp.concatenate([xr * hr - xi * hi, xr * hi + xi * hr], axis=0).astype(BF)
        skip = skip_ref[:, cols]
        mixed = nn(inv1_ref[...], y)[:out_rows] + skip * kv[k, span : span + out_rows]
        g = nn(fwd_ref[...], gm[k].astype(BF))
        gr, gi = g[:half], g[half:]
        w = jnp.concatenate([gr * hr + gi * hi, gi * hr - gr * hi], axis=0).astype(BF)
        grad_kv = nn(inv2_ref[...], w)[:out_rows] + skip * gm[k, 0:out_rows]
        cot_ext = jnp.concatenate([cot[:, cols].astype(F32), from_next[3, :, cols]], axis=0)
        table = sketch[:, cols]
        for s in range(3):
            if s == 0:
                shift[0:out_rows] = cot_ext * mixed
            elif s == 1:
                shift[0:out_rows] = grad_kv * fv[k]
            else:
                shift[0:out_rows] = grad_kv * fk[k]
            coeff = short_ref[s, :, cols]
            running = coeff[0:1] * shift[0:rows]
            for j in range(1, taps):
                running = running + coeff[j : j + 1] * shift[j : j + rows]
            joined = jnp.concatenate([up[s, :, cols], table], axis=0)
            prods[s] += nt(running.astype(BF), joined)
        return carry

    lax.fori_loop(0, chunks, streams_back, 0)

    for i, copy in enumerate(psk_copies[1]):
        copy.wait_recv()
        psk_copies[2][i + 1].start()
    for copy in psk_copies[2]:
        copy.wait_recv()
    flatten(ptab, pflat)
    words_p = pflat[...]
    high_p = words_p.astype(BF)
    rest_p = (words_p - high_p.astype(F32)).astype(BF)
    picked = psk[...]
    token_sketch = (nn(picked, high_p) + nn(picked, rest_p))[RIM : RIM + rows, 0:BUCKETS]
    for s in range(3):
        block = slice(s * rank, (s + 1) * rank)
        done[0:BUCKETS, block] = ADAPTER_SCALE * tn(token_sketch, prods[s, :, 0:rank])
        done[BUCKETS : 2 * BUCKETS, block] = tn(
            prods[s, :, rank:], low[RIM : RIM + rows, block].astype(F32)
        )

    few = 2 * BUCKETS // ns
    for i in range(ns):
        part[i] = done[i * few : (i + 1) * few]
    got_s[s_me] = part[s_me]
    spread = [
        remote(
            part.at[lax.rem(s_me + d, ns)],
            got_s.at[s_me],
            fin_send.at[0, d - 1],
            fin_recv.at[0, d - 1],
            {"seq": lax.rem(s_me + d, ns)},
        )
        for d in range(1, ns)
    ]

    def finish(copies):
        for copy in copies:
            copy.start()
        for copy in copies:
            copy.wait_recv()

    def added(buffer, count):
        total = buffer[0]
        for i in range(1, count):
            total = total + buffer[i]
        return total

    finish(spread)
    got_z[z_me] = added(got_s, ns)
    along = [
        remote(
            got_z.at[z_me],
            got_z.at[z_me],
            fz_send.at[d - 1],
            fz_recv.at[d - 1],
            {"tensor": lax.rem(z_me + d, nz)},
        )
        for d in range(1, nz)
    ]
    finish(along)
    for copy in spread:
        copy.wait_send()
    part[s_me] = added(got_z, nz)
    back = [
        remote(
            part.at[s_me],
            full_sum.at[s_me],
            fin_send.at[1, d - 1],
            fin_recv.at[1, d - 1],
            {"seq": lax.rem(s_me + d, ns)},
        )
        for d in range(1, ns)
    ]
    full_sum[s_me] = part[s_me]
    finish(back)
    for i in range(ns):
        done[i * few : (i + 1) * few] = full_sum[i]
    raw = done[...]
    mean = jnp.sum(raw * raw) / (2 * BUCKETS * wide)
    features = raw * lax.rsqrt(jnp.full((1, wide), FEATURE_EPS, F32) + mean)
    out_ref[0] = features[:BUCKETS]
    out_ref[1] = features[BUCKETS:]

    pending = scatters + along + back
    for group in low_copies + psk_copies:
        pending = pending + group
    for copy in pending:
        copy.wait_send()

    @pl.when(has_next)
    def _():
        ids_to_next.wait_send()
        rim_to_next.wait_send()

        def drain(k, carry):
            kv_copy(k).wait_send()
            return carry

        lax.fori_loop(0, chunks, drain, 0)

    @pl.when(has_prev)
    def _():
        ids_to_prev.wait_send()
        rim_to_prev.wait_send()

        def drain(k, carry):
            gm_copy(k).wait_send()
            return carry

        lax.fori_loop(0, chunks, drain, 0)


def on_device(
    npart,
    ns,
    nz,
    token_ids,
    embed,
    norm_gain_vector,
    base_proj,
    adapter_down_matrices,
    adapter_up_matrices,
    short_taps,
    medium_taps,
    skip_gain,
    mixer_cot,
    bucket_ids,
):
    rows = token_ids.shape[0]
    vocab, width = embed.shape
    rank = adapter_up_matrices.shape[1]
    span = medium_taps.shape[0]
    wide = 3 * rank
    chunks = width // CHUNK
    fwd, inv1, inv2 = spectrum_tables(rows, span)
    ext = fwd.shape[1]
    out_rows = rows + RIM
    padded = ceil_to(rows + 2 * RIM, 16)
    words = vocab // (npart * ns)
    own = words // nz
    peers = npart * ns // 2
    few = 2 * BUCKETS // ns
    ids = jnp.broadcast_to(token_ids[:, None] + 1, (rows, 128))
    vmem = pl.BlockSpec(memory_space=pltpu.VMEM)
    any_space = pl.BlockSpec(memory_space=pl.ANY)
    dma = pltpu.SemaphoreType.DMA
    return pl.pallas_call(
        functools.partial(kernel, npart, ns, nz),
        out_shape=jax.ShapeDtypeStruct((2, BUCKETS, wide), F32),
        in_specs=[vmem] + [any_space] * 13,
        out_specs=vmem,
        scratch_shapes=[
            pltpu.VMEM((words, width), BF),
            pltpu.VMEM((1, width), F32),
            pltpu.VMEM((3, rows, width), BF),
            pltpu.VMEM((width, wide), BF),
            pltpu.VMEM((3, rank, width), BF),
            pltpu.VMEM(short_taps.shape, F32),
            pltpu.VMEM((span, width), F32),
            pltpu.VMEM((1, width), F32),
            pltpu.VMEM((rows, width), BF),
            pltpu.VMEM((1, width), jnp.int32),
            pltpu.VMEM(fwd.shape, BF),
            pltpu.VMEM(inv1.shape, BF),
            pltpu.VMEM(inv2.shape, BF),
            pltpu.VMEM((padded, 128), jnp.int32),
            pltpu.VMEM((BUCKETS, width), BF),
            pltpu.VMEM((4, RIM, width), F32),
            pltpu.VMEM((3, RIM, width), F32),
            pltpu.VMEM((4, RIM, width), F32),
            pltpu.VMEM((3, RIM, width), F32),
            pltpu.VMEM((nz, own, wide + 128), F32),
            pltpu.VMEM((words, wide + 128), F32),
            pltpu.VMEM((nz - 1, own, wide + 128), F32),
            pltpu.VMEM((npart, ns, nz, own, wide), F32),
            pltpu.VMEM((npart, ns, nz, own, 128), F32),
            pltpu.VMEM((vocab, wide), F32),
            pltpu.VMEM((vocab, 128), F32),
            pltpu.VMEM((padded, wide), BF),
            pltpu.VMEM((padded, vocab), BF),
            pltpu.VMEM((chunks, fwd.shape[0], CHUNK), F32),
            pltpu.VMEM((chunks, ext, CHUNK), F32),
            pltpu.VMEM((chunks, ext, CHUNK), F32),
            pltpu.VMEM((chunks, out_rows, CHUNK), F32),
            pltpu.VMEM((chunks, out_rows, CHUNK), F32),
            pltpu.VMEM((padded, CHUNK), F32),
            pltpu.VMEM((3, rows, rank + BUCKETS), F32),
            pltpu.VMEM((ns, few, wide), F32),
            pltpu.VMEM((ns, few, wide), F32),
            pltpu.VMEM((nz, few, wide), F32),
            pltpu.VMEM((ns, few, wide), F32),
            pltpu.VMEM((2 * BUCKETS, wide), F32),
            dma((13,)),
            dma((4,)),
            dma((4,)),
            dma((nz - 1,)),
            dma((nz - 1,)),
            dma((2, nz - 1)),
            dma((2, nz - 1)),
            dma((2, peers - 1)),
            dma((2, peers - 1)),
            dma((2, peers)),
            dma((2, peers)),
            dma((chunks,)),
            dma((chunks,)),
            dma((chunks,)),
            dma((chunks,)),
            dma((2, ns - 1)),
            dma((2, ns - 1)),
            dma((nz - 1,)),
            dma((nz - 1,)),
        ],
        compiler_params=pltpu.CompilerParams(
            collective_id=0, has_side_effects=True, vmem_limit_bytes=58 * 1024 * 1024
        ),
    )(
        ids,
        embed,
        norm_gain_vector[None],
        base_proj,
        adapter_down_matrices,
        adapter_up_matrices,
        short_taps,
        medium_taps,
        skip_gain[None],
        mixer_cot,
        bucket_ids[None],
        jnp.asarray(fwd, BF),
        jnp.asarray(inv1, BF),
        jnp.asarray(inv2, BF),
    )


def solution(mesh):
    in_specs = (
        P(("parts", "seq")),
        P(None, "tensor"),
        P("tensor"),
        P(None, ("parts", "seq"), "tensor"),
        P("tensor", None),
        P(None, None, "tensor"),
        P(None, None, "tensor"),
        P(None, "tensor"),
        P("tensor"),
        P(("parts", "seq"), "tensor"),
        P("tensor"),
    )
    return jax.shard_map(
        functools.partial(
            on_device, mesh.shape["parts"], mesh.shape["seq"], mesh.shape["tensor"]
        ),
        mesh=mesh,
        in_specs=in_specs,
        out_specs=P("parts", None, None),
        check_vma=False,
    )
```

```python
import functools

import jax
import jax.numpy as jnp
import numpy as np
from jax import lax
from jax.experimental import pallas as pl
from jax.experimental.pallas import tpu as pltpu
from jax.sharding import PartitionSpec as P

BUCKETS = 16
NORM_EPS = 1e-05
FEATURE_EPS = 1e-06
ADAPTER_SCALE = 1.5
RIM = 8
CHUNK = 256
BLOCK = 64
BF = jnp.bfloat16
F32 = jnp.float32
HIGHEST = lax.Precision.HIGHEST
MESH = pl.DeviceIdType.MESH


def ceil_to(count, step):
    return -(-count // step) * step


def spectrum_tables(rows, span):
    ext = ceil_to(rows + RIM + span, 16)
    half = ceil_to(ext, 32) // 2
    period = 2 * half
    omega = 2.0 * np.pi * (np.arange(half) + 0.5) / period
    angle = omega[:, None] * np.arange(ext + 16)[None, :]
    fwd = np.concatenate([np.cos(angle), -np.sin(angle)], axis=0)
    inv = fwd.T * (2.0 / period)
    out_rows = ceil_to(rows + RIM, 16)
    return fwd[:, :ext], inv[span : span + out_rows], inv[:out_rows]


def nn(a, b):
    return jnp.dot(a, b, preferred_element_type=F32)


def nt(a, b):
    return lax.dot_general(a, b, (((1,), (1,)), ((), ())), preferred_element_type=F32)


def tn(a, b):
    return lax.dot_general(
        a, b, (((0,), (0,)), ((), ())), precision=HIGHEST, preferred_element_type=F32
    )


def kernel(
    npart,
    ns,
    nz,
    ids_ref,
    embed_hbm,
    gain_hbm,
    base_hbm,
    down_hbm,
    up_hbm,
    short_hbm,
    medium_hbm,
    skip_hbm,
    cot_hbm,
    bucket_hbm,
    fwd_hbm,
    inv1_hbm,
    inv2_hbm,
    out_ref,
    embed_own,
    gain_ref,
    base,
    down_ref,
    up,
    short_ref,
    medium_ref,
    skip_ref,
    cot,
    bucket_ref,
    fwd_ref,
    inv1_ref,
    inv2_ref,
    ids_ext,
    sketch,
    to_prev,
    to_next,
    from_next,
    from_prev,
    acc,
    sums,
    rs,
    tab,
    ptab,
    flat,
    pflat,
    low,
    psk,
    spec,
    kv,
    gm,
    fk,
    fv,
    shift,
    spectra,
    grads,
    prods,
    part,
    got_s,
    got_z,
    full_sum,
    done,
    load_sem,
    rim_send,
    rim_recv,
    rs_send,
    rs_recv,
    ag_send,
    ag_recv,
    pl_send,
    pl_recv,
    sib_send,
    sib_recv,
    kv_send,
    kv_recv,
    gm_send,
    gm_recv,
    fin_send,
    fin_recv,
    fz_send,
    fz_recv,
):
    rows = ids_ref.shape[0]
    vocab, width = embed_hbm.shape
    rank = up_hbm.shape[1]
    span = medium_ref.shape[0]
    taps = short_ref.shape[1]
    padded = ids_ext.shape[0]
    words = embed_own.shape[0]
    own = words // nz
    out_rows = rows + RIM
    all_rows = rows + 2 * RIM
    ext = kv.shape[1]
    half = fwd_ref.shape[0] // 2
    chunks = width // CHUNK
    wide = 3 * rank
    s_me = lax.axis_index("seq")
    z_me = lax.axis_index("tensor")
    p_me = lax.axis_index("parts")
    core = lax.rem(s_me, 2)
    sibling = {"seq": s_me + 1 - 2 * core}
    has_prev = s_me > 0
    has_next = s_me < ns - 1
    prev = {"seq": lax.rem(s_me + ns - 1, ns)}
    succ = {"seq": lax.rem(s_me + 1, ns)}

    first_word = pl.multiple_of((p_me * ns + s_me) * words, words)
    loads = [
        pltpu.make_async_copy(src, dst, load_sem.at[i])
        for i, (src, dst) in enumerate(
            [
                (embed_hbm.at[pl.ds(first_word, words)], embed_own),
                (gain_hbm, gain_ref),
                (bucket_hbm, bucket_ref),
                (down_hbm, down_ref),
                (base_hbm, base),
                (cot_hbm, cot),
                (fwd_hbm, fwd_ref),
                (medium_hbm, medium_ref),
                (up_hbm, up),
                (short_hbm, short_ref),
                (skip_hbm, skip_ref),
                (inv1_hbm, inv1_ref),
                (inv2_hbm, inv2_ref),
            ]
        )
    ]
    for load in loads:
        load.start()

    barrier = pltpu.get_barrier_semaphore()
    for d in range(1, ns):
        pl.semaphore_signal(
            barrier, inc=1, device_id={"seq": lax.rem(s_me + d, ns)}, device_id_type=MESH
        )
    for d in range(1, nz):
        pl.semaphore_signal(
            barrier, inc=1, device_id={"tensor": lax.rem(z_me + d, nz)}, device_id_type=MESH
        )
    plane = [(dp, ds) for dp in range(npart) for ds in range(0, ns, 2)][1:]

    def plane_peer(dp, ds):
        return lax.rem(p_me + dp, npart), lax.rem(s_me + ds, ns)

    away = [(dp, ds) for dp, ds in plane if dp > 0]
    for dp, ds in away:
        p_to, s_to = plane_peer(dp, ds)
        pl.semaphore_signal(
            barrier, inc=1, device_id={"parts": p_to, "seq": s_to}, device_id_type=MESH
        )
    pl.semaphore_wait(barrier, ns + nz - 2 + len(away))

    def remote(src, dst, send, recv, device):
        return pltpu.make_async_remote_copy(
            src_ref=src,
            dst_ref=dst,
            send_sem=send,
            recv_sem=recv,
            device_id=device,
            device_id_type=MESH,
        )

    ids_to_next = remote(
        ids_ref.at[rows - RIM : rows], ids_ext.at[0:RIM], rim_send.at[0], rim_recv.at[0], succ
    )
    ids_to_prev = remote(
        ids_ref.at[0:RIM],
        ids_ext.at[RIM + rows : all_rows],
        rim_send.at[1],
        rim_recv.at[1],
        prev,
    )
    rim_to_next = remote(to_next, from_prev, rim_send.at[2], rim_recv.at[2], succ)
    rim_to_prev = remote(to_prev, from_next, rim_send.at[3], rim_recv.at[3], prev)

    @pl.when(has_next)
    def _():
        ids_to_next.start()

    @pl.when(has_prev)
    def _():
        ids_to_prev.start()

    @pl.when(jnp.logical_not(has_prev))
    def _():
        ids_ext[0:RIM] = jnp.zeros((RIM, 128), jnp.int32)
        from_prev[...] = jnp.zeros_like(from_prev)
        for k in range(chunks):
            kv[k, 0:span] = jnp.zeros((span, CHUNK), F32)

    @pl.when(jnp.logical_not(has_next))
    def _():
        ids_ext[RIM + rows : all_rows] = jnp.zeros((RIM, 128), jnp.int32)
        from_next[...] = jnp.zeros_like(from_next)
        for k in range(chunks):
            gm[k, rows : rows + span + RIM] = jnp.zeros((span + RIM, CHUNK), F32)

    tail = ext - (out_rows + span)
    if tail:
        for k in range(chunks):
            kv[k, ext - tail : ext] = jnp.zeros((tail, CHUNK), F32)
            gm[k, ext - tail : ext] = jnp.zeros((tail, CHUNK), F32)
    if padded > all_rows:
        ids_ext[all_rows:padded] = jnp.zeros((padded - all_rows, 128), jnp.int32)
    ids_ext[RIM : RIM + rows] = ids_ref[...]
    for load in loads[:4]:
        load.wait()
    bucket = bucket_ref[...]
    hit = lax.broadcasted_iota(jnp.int32, (BUCKETS, width), 0) == jnp.bitwise_and(
        bucket, BUCKETS - 1
    )
    sign = jnp.where(bucket >= BUCKETS, -1.0, 1.0).astype(F32)
    sketch[...] = jnp.where(hit, sign, 0.0).astype(BF)
    sums[...] = jnp.zeros_like(sums)

    def at(k):
        return pl.ds(pl.multiple_of(k * CHUNK, CHUNK), CHUNK)

    def front(k, carry):
        cols = at(k)
        x = embed_own[:, cols].astype(F32)
        squares = jnp.sum(x * x, axis=1, keepdims=True)
        gained = x * gain_ref[:, cols]
        high = gained.astype(BF)
        rest = (gained - high.astype(F32)).astype(BF)
        weights = down_ref[cols, :]
        sums[:, :wide] += nn(high, weights) + nn(rest, weights)
        table = sketch[:, cols]
        sums[:, wide : wide + BUCKETS] += nt(high, table) + nt(rest, table)
        sums[:, wide + BUCKETS : wide + BUCKETS + 1] += squares
        return carry

    lax.fori_loop(0, chunks, front, 0)

    for z in range(nz):
        acc[z] = sums[z * own : (z + 1) * own]
    scatters = []
    for d in range(1, nz):
        z_to = lax.rem(z_me + d, nz)
        scatters.append(
            remote(
                acc.at[z_to],
                rs.at[d - 1],
                rs_send.at[d - 1],
                rs_recv.at[d - 1],
                {"tensor": z_to},
            )
        )
    for copy in scatters:
        copy.start()

    loads[4].wait()
    loads[5].wait()
    for s in range(3):
        to_prev[s] = base[s, 0 : 2 * RIM].astype(F32)[:RIM]
        to_next[s] = base[s, rows - 2 * RIM : rows].astype(F32)[RIM:]
    to_prev[3] = cot[0 : 2 * RIM].astype(F32)[:RIM]

    @pl.when(has_next)
    def _():
        rim_to_next.start()

    @pl.when(has_prev)
    def _():
        rim_to_prev.start()


    total = acc[z_me]
    for d in range(1, nz):
        scatters[d - 1].wait_recv()
        total = total + rs[d - 1]
    scale = lax.rsqrt(
        total[:, wide + BUCKETS : wide + BUCKETS + 1] / (width * nz) + NORM_EPS
    )
    tab[p_me, s_me, z_me] = (total[:, :wide] * (scale * ADAPTER_SCALE)).astype(BF).astype(F32)
    ptab[p_me, s_me, z_me] = total[:, wide:] * scale

    def hand_out(which, buffer):
        lines, planes, siblings = [], [], []
        block = buffer.at[p_me, s_me, z_me]
        for d in range(1, nz):
            lines.append(
                remote(
                    block,
                    block,
                    ag_send.at[which, d - 1],
                    ag_recv.at[which, d - 1],
                    {"tensor": lax.rem(z_me + d, nz)},
                )
            )
        block = buffer.at[p_me, s_me]
        for i, (dp, ds) in enumerate(plane):
            p_to, s_to = plane_peer(dp, ds)
            planes.append(
                remote(
                    block,
                    block,
                    pl_send.at[which, i],
                    pl_recv.at[which, i],
                    {"parts": p_to, "seq": s_to},
                )
            )
        for i, (dp, ds) in enumerate([(0, 0)] + plane):
            p_of, s_of = lax.rem(p_me + npart - dp, npart), lax.rem(s_me + ns - ds, ns)
            block = buffer.at[p_of, s_of]
            siblings.append(
                remote(block, block, sib_send.at[which, i], sib_recv.at[which, i], sibling)
            )
        return lines, planes, siblings

    low_copies = hand_out(0, tab)
    psk_copies = hand_out(1, ptab)
    for copy in low_copies[0]:
        copy.start()
    for copy in psk_copies[0]:
        copy.start()

    for load in loads[6:]:
        load.wait()

    def filter_spectrum(k, carry):
        spec[k] = nn(fwd_ref[:, :span], medium_ref[:, at(k)].astype(BF))
        return carry

    for copy in low_copies[0]:
        copy.wait_recv()
    for copy in low_copies[1]:
        copy.start()
    low_copies[2][0].start()

    lax.fori_loop(0, chunks, filter_spectrum, 0)

    @pl.when(has_prev)
    def _():
        ids_to_next.wait_recv()
        rim_to_next.wait_recv()

    @pl.when(has_next)
    def _():
        ids_to_prev.wait_recv()
        rim_to_prev.wait_recv()

    ids = jnp.concatenate([ids_ext[...]] * (vocab // 128), axis=1)
    one_hot = jnp.where(
        ids == lax.broadcasted_iota(jnp.int32, (padded, vocab), 1) + 1, 1.0, 0.0
    ).astype(BF)

    for i, copy in enumerate(low_copies[1]):
        copy.wait_recv()
        low_copies[2][i + 1].start()
    for copy in psk_copies[0]:
        copy.wait_recv()
    for copy in psk_copies[1]:
        copy.start()
    psk_copies[2][0].start()
    for copy in low_copies[2]:
        copy.wait_recv()

    def flatten(buffer, target):
        for p in range(npart):
            for q in range(ns):
                for z in range(nz):
                    begin = ((p * ns + q) * nz + z) * own
                    target[begin : begin + own] = buffer[p, q, z]

    flatten(tab, flat)
    psk[...] = one_hot
    low[...] = nn(one_hot, flat[...].astype(BF)).astype(BF)

    blocks = [(r, BLOCK) for r in range(0, rows, BLOCK)] + [(rows, RIM)]

    def kv_copy(k):
        return remote(
            kv.at[k, rows : rows + span], kv.at[k, 0:span], kv_send.at[k], kv_recv.at[k], succ
        )

    def gm_copy(k):
        return remote(
            gm.at[k, 0 : span + RIM],
            gm.at[k, rows : rows + span + RIM],
            gm_send.at[k],
            gm_recv.at[k],
            prev,
        )

    def streams_in(k, carry):
        cols = at(k)
        for s in range(3):
            mixed_in = nn(low[0:all_rows, s * rank : (s + 1) * rank], up[s, :, cols])
            shift[0, s, 0:RIM] = from_prev[s, :, cols] + mixed_in[:RIM]
            for r in range(0, rows, BLOCK):
                shift[0, s, RIM + r : RIM + r + BLOCK] = (
                    base[s, r : r + BLOCK, cols].astype(F32) + mixed_in[RIM + r : RIM + r + BLOCK]
                )
            shift[0, s, RIM + rows : all_rows] = from_next[s, :, cols] + mixed_in[RIM + rows :]

        def causal(s, r, count):
            coeff = short_ref[s, :, cols]
            running = coeff[0:1] * shift[0, s, RIM + r : RIM + r + count]
            for j in range(1, taps):
                begin = RIM - j + r
                running = running + coeff[j : j + 1] * shift[0, s, begin : begin + count]
            return running

        for r, count in blocks:
            fk_part = causal(1, r, count)
            fv_part = causal(2, r, count)
            fk[k, r : r + count] = fk_part
            fv[k, r : r + count] = fv_part
            kv[k, span + r : span + r + count] = fk_part * fv_part
            if r < rows:
                gm[k, r : r + count] = cot[r : r + count, cols].astype(F32) * causal(0, r, count)

        @pl.when(has_next)
        def _():
            kv_copy(k).start()

        @pl.when(has_prev)
        def _():
            gm_copy(k).start()

        return carry

    lax.fori_loop(0, chunks, streams_in, 0)

    def streams_back(pair, carry):
        @pl.when(has_prev)
        def _():
            for u in range(2):
                kv_copy(2 * pair + u).wait_recv()

        @pl.when(has_next)
        def _():
            for u in range(2):
                gm_copy(2 * pair + u).wait_recv()

        for u in range(2):
            k = 2 * pair + u
            cols = at(k)
            skip = skip_ref[:, cols]
            x = nn(fwd_ref[...], kv[k].astype(BF))
            g = nn(fwd_ref[...], gm[k].astype(BF))
            for r in range(0, half, 16):
                upper, lower = slice(r, r + 16), slice(half + r, half + r + 16)
                hr, hi = spec[k, upper], spec[k, lower]
                xr, xi = x[upper], x[lower]
                spectra[u, 0, upper] = (xr * hr - xi * hi).astype(BF)
                spectra[u, 0, lower] = (xr * hi + xi * hr).astype(BF)
                gr, gi = g[upper], g[lower]
                spectra[u, 1, upper] = (gr * hr + gi * hi).astype(BF)
                spectra[u, 1, lower] = (gi * hr - gr * hi).astype(BF)
            mixed = nn(inv1_ref[...], spectra[u, 0])
            grad_kv = nn(inv2_ref[...], spectra[u, 1])
            for r, count in blocks:
                here = slice(r, r + count)
                mixed_part = mixed[here] + skip * kv[k, span + r : span + r + count]
                grad_part = grad_kv[here] + skip * gm[k, here]
                if r < rows:
                    cot_part = cot[here, cols].astype(F32)
                else:
                    cot_part = from_next[3, :, cols]
                shift[u, 0, here] = cot_part * mixed_part
                shift[u, 1, here] = grad_part * fv[k, here]
                shift[u, 2, here] = grad_part * fk[k, here]
            for s in range(3):
                coeff = short_ref[s, :, cols]
                for r in range(0, rows, BLOCK):
                    running = coeff[0:1] * shift[u, s, r : r + BLOCK]
                    for j in range(1, taps):
                        running = running + coeff[j : j + 1] * shift[u, s, r + j : r + j + BLOCK]
                    grads[s, r : r + BLOCK, cols] = running.astype(BF)
        return carry

    lax.fori_loop(0, chunks // 2, streams_back, 0)
    for s in range(3):
        prods[s] = nt(grads[s], jnp.concatenate([up[s], sketch[...]], axis=0))

    for i, copy in enumerate(psk_copies[1]):
        copy.wait_recv()
        psk_copies[2][i + 1].start()
    for copy in psk_copies[2]:
        copy.wait_recv()
    flatten(ptab, pflat)
    words_p = pflat[...]
    high_p = words_p.astype(BF)
    rest_p = (words_p - high_p.astype(F32)).astype(BF)
    picked = psk[...]
    token_sketch = (nn(picked, high_p) + nn(picked, rest_p))[RIM : RIM + rows, 0:BUCKETS]
    for s in range(3):
        block = slice(s * rank, (s + 1) * rank)
        done[0:BUCKETS, block] = ADAPTER_SCALE * tn(token_sketch, prods[s, :, 0:rank])
        done[BUCKETS : 2 * BUCKETS, block] = tn(
            prods[s, :, rank:], low[RIM : RIM + rows, block].astype(F32)
        )

    few = 2 * BUCKETS // ns
    for i in range(ns):
        part[i] = done[i * few : (i + 1) * few]
    got_s[s_me] = part[s_me]
    spread = [
        remote(
            part.at[lax.rem(s_me + d, ns)],
            got_s.at[s_me],
            fin_send.at[0, d - 1],
            fin_recv.at[0, d - 1],
            {"seq": lax.rem(s_me + d, ns)},
        )
        for d in range(1, ns)
    ]

    def finish(copies):
        for copy in copies:
            copy.start()
        for copy in copies:
            copy.wait_recv()

    def added(buffer, count):
        total = buffer[0]
        for i in range(1, count):
            total = total + buffer[i]
        return total

    finish(spread)
    got_z[z_me] = added(got_s, ns)
    along = [
        remote(
            got_z.at[z_me],
            got_z.at[z_me],
            fz_send.at[d - 1],
            fz_recv.at[d - 1],
            {"tensor": lax.rem(z_me + d, nz)},
        )
        for d in range(1, nz)
    ]
    finish(along)
    for copy in spread:
        copy.wait_send()
    part[s_me] = added(got_z, nz)
    back = [
        remote(
            part.at[s_me],
            full_sum.at[s_me],
            fin_send.at[1, d - 1],
            fin_recv.at[1, d - 1],
            {"seq": lax.rem(s_me + d, ns)},
        )
        for d in range(1, ns)
    ]
    full_sum[s_me] = part[s_me]
    finish(back)
    for i in range(ns):
        done[i * few : (i + 1) * few] = full_sum[i]
    raw = done[...]
    mean = jnp.sum(raw * raw) / (2 * BUCKETS * wide)
    features = raw * lax.rsqrt(jnp.full((1, wide), FEATURE_EPS, F32) + mean)
    out_ref[0] = features[:BUCKETS]
    out_ref[1] = features[BUCKETS:]

    pending = scatters + along + back
    for group in low_copies + psk_copies:
        pending = pending + group
    for copy in pending:
        copy.wait_send()

    @pl.when(has_next)
    def _():
        ids_to_next.wait_send()
        rim_to_next.wait_send()

        def drain(k, carry):
            kv_copy(k).wait_send()
            return carry

        lax.fori_loop(0, chunks, drain, 0)

    @pl.when(has_prev)
    def _():
        ids_to_prev.wait_send()
        rim_to_prev.wait_send()

        def drain(k, carry):
            gm_copy(k).wait_send()
            return carry

        lax.fori_loop(0, chunks, drain, 0)


def on_device(
    npart,
    ns,
    nz,
    token_ids,
    embed,
    norm_gain_vector,
    base_proj,
    adapter_down_matrices,
    adapter_up_matrices,
    short_taps,
    medium_taps,
    skip_gain,
    mixer_cot,
    bucket_ids,
):
    rows = token_ids.shape[0]
    vocab, width = embed.shape
    rank = adapter_up_matrices.shape[1]
    span = medium_taps.shape[0]
    wide = 3 * rank
    chunks = width // CHUNK
    fwd, inv1, inv2 = spectrum_tables(rows, span)
    ext = fwd.shape[1]
    out_rows = rows + RIM
    padded = ceil_to(rows + 2 * RIM, 16)
    words = vocab // (npart * ns)
    own = words // nz
    peers = npart * ns // 2
    few = 2 * BUCKETS // ns
    ids = jnp.broadcast_to(token_ids[:, None] + 1, (rows, 128))
    vmem = pl.BlockSpec(memory_space=pltpu.VMEM)
    any_space = pl.BlockSpec(memory_space=pl.ANY)
    dma = pltpu.SemaphoreType.DMA
    return pl.pallas_call(
        functools.partial(kernel, npart, ns, nz),
        out_shape=jax.ShapeDtypeStruct((2, BUCKETS, wide), F32),
        in_specs=[vmem] + [any_space] * 13,
        out_specs=vmem,
        scratch_shapes=[
            pltpu.VMEM((words, width), BF),
            pltpu.VMEM((1, width), F32),
            pltpu.VMEM((3, rows, width), BF),
            pltpu.VMEM((width, wide), BF),
            pltpu.VMEM((3, rank, width), BF),
            pltpu.VMEM(short_taps.shape, F32),
            pltpu.VMEM((span, width), F32),
            pltpu.VMEM((1, width), F32),
            pltpu.VMEM((rows, width), BF),
            pltpu.VMEM((1, width), jnp.int32),
            pltpu.VMEM(fwd.shape, BF),
            pltpu.VMEM(inv1.shape, BF),
            pltpu.VMEM(inv2.shape, BF),
            pltpu.VMEM((padded, 128), jnp.int32),
            pltpu.VMEM((BUCKETS, width), BF),
            pltpu.VMEM((4, RIM, width), F32),
            pltpu.VMEM((3, RIM, width), F32),
            pltpu.VMEM((4, RIM, width), F32),
            pltpu.VMEM((3, RIM, width), F32),
            pltpu.VMEM((nz, own, wide + 128), F32),
            pltpu.VMEM((words, wide + 128), F32),
            pltpu.VMEM((nz - 1, own, wide + 128), F32),
            pltpu.VMEM((npart, ns, nz, own, wide), F32),
            pltpu.VMEM((npart, ns, nz, own, 128), F32),
            pltpu.VMEM((vocab, wide), F32),
            pltpu.VMEM((vocab, 128), F32),
            pltpu.VMEM((padded, wide), BF),
            pltpu.VMEM((padded, vocab), BF),
            pltpu.VMEM((chunks, fwd.shape[0], CHUNK), F32),
            pltpu.VMEM((chunks, ext, CHUNK), F32),
            pltpu.VMEM((chunks, ext, CHUNK), F32),
            pltpu.VMEM((chunks, out_rows, CHUNK), F32),
            pltpu.VMEM((chunks, out_rows, CHUNK), F32),
            pltpu.VMEM((2, 3, padded, CHUNK), F32),
            pltpu.VMEM((2, 2, fwd.shape[0], CHUNK), BF),
            pltpu.VMEM((3, rows, width), BF),
            pltpu.VMEM((3, rows, rank + BUCKETS), F32),
            pltpu.VMEM((ns, few, wide), F32),
            pltpu.VMEM((ns, few, wide), F32),
            pltpu.VMEM((nz, few, wide), F32),
            pltpu.VMEM((ns, few, wide), F32),
            pltpu.VMEM((2 * BUCKETS, wide), F32),
            dma((13,)),
            dma((4,)),
            dma((4,)),
            dma((nz - 1,)),
            dma((nz - 1,)),
            dma((2, nz - 1)),
            dma((2, nz - 1)),
            dma((2, peers - 1)),
            dma((2, peers - 1)),
            dma((2, peers)),
            dma((2, peers)),
            dma((chunks,)),
            dma((chunks,)),
            dma((chunks,)),
            dma((chunks,)),
            dma((2, ns - 1)),
            dma((2, ns - 1)),
            dma((nz - 1,)),
            dma((nz - 1,)),
        ],
        compiler_params=pltpu.CompilerParams(
            collective_id=0, has_side_effects=True, vmem_limit_bytes=58 * 1024 * 1024
        ),
    )(
        ids,
        embed,
        norm_gain_vector[None],
        base_proj,
        adapter_down_matrices,
        adapter_up_matrices,
        short_taps,
        medium_taps,
        skip_gain[None],
        mixer_cot,
        bucket_ids[None],
        jnp.asarray(fwd, BF),
        jnp.asarray(inv1, BF),
        jnp.asarray(inv2, BF),
    )


def solution(mesh):
    in_specs = (
        P(("parts", "seq")),
        P(None, "tensor"),
        P("tensor"),
        P(None, ("parts", "seq"), "tensor"),
        P("tensor", None),
        P(None, None, "tensor"),
        P(None, None, "tensor"),
        P(None, "tensor"),
        P("tensor"),
        P(("parts", "seq"), "tensor"),
        P("tensor"),
    )
    return jax.shard_map(
        functools.partial(
            on_device, mesh.shape["parts"], mesh.shape["seq"], mesh.shape["tensor"]
        ),
        mesh=mesh,
        in_specs=in_specs,
        out_specs=P("parts", None, None),
        check_vma=False,
    )
```
